256 devices in a mesh: dp: 8 (over z), tensor: 8 (over y, x_hi), seq: 4 (over x_lo, core).
Axes of the slice: x: 4 (x_hi: 2, x_lo: 2; x = x_hi * 2 + x_lo), y: 4, z: 8, core: 2. Of those that a mesh axis runs over, the one named last changes fastest.
Arguments:
- train_act: bfloat16 [8, 4096, 8192], P('dp', 'seq', 'tensor'), may hold values from -0.796875 to 0.796875
- train_grad: bfloat16 [8, 4096, 28672], P('dp', 'seq', 'tensor'), may hold values from -0.59765625 to 0.59765625
- val_act: bfloat16 [1024, 8192], P('dp', 'tensor'), may hold values from -0.796875 to 0.796875
- val_grad: bfloat16 [1024, 28672], P('dp', 'tensor'), may hold values from -0.59765625 to 0.59765625
- val_mask: int32 [1024], P('dp'), may hold values 0 or 1
- lengths: int32 [8], P('dp'), may hold values from 1024 to 4096
Outputs:
- token_values: float32 [8, 4096], P('dp', 'seq')
- example_values: float32 [8], P('dp')
The draws below stay inside these ranges and needn't reach their ends.
All inputs are finite; a program needn't handle non-finite values. No bound on the sum of `val_mask` on one device may be relied on, other than what follows from the above.
Results may differ from the reference program's by a relative error of at most 0.0003.
Values may be sent and summed in bfloat16 or wider, within the bound.
No kernel may reach another device: no remote copies, remote signals or barrier semaphores. Data moves between devices by JAX's collectives and lax.ppermute only.
A program may use at most 128 MiB of HBM per device.

```python
import jax
import jax.numpy as jnp
from jax import lax

D = 8192
FF = 28672
SEQ_LEN = 4096
SEQS = 8
VAL = 1024


def set_ends(result, key, least, high):
    longest = result.shape.index(max(result.shape))
    spots = []
    for shift in (0, 1):
        where = [jax.random.randint(jax.random.fold_in(key, axis), (), 0, length) for axis, length in enumerate(result.shape)]
        where[longest] = (where[longest] + shift) % result.shape[longest]
        spots.append(tuple(where))
    return result.at[spots[0]].set(least).at[spots[1]].set(high)


def block_levels(stream_key, extent, split, low, largest):
    factor_of, own = 1.0, jax.random.fold_in(stream_key, 6)
    for position, blocks in split:
        draws = jnp.exp(jax.random.uniform(jax.random.fold_in(own, position), (blocks,), jnp.float32, low / len(split), largest / len(split)))
        factor_of = factor_of * jnp.repeat(draws, extent[position] // blocks).reshape([-1 if axis == position else 1 for axis in range(len(extent))])
    return factor_of


def scatter_about(key, shape, width, limit, pieces=(), dtype=jnp.bfloat16):
    level = block_levels(key, shape, pieces, -0.22, 0.18) if pieces else 1.0
    entries = jax.random.normal(key, shape, jnp.float32) * width * level
    return jnp.minimum(jnp.maximum(entries, -limit), limit).astype(dtype)


def setup_inputs(seed: int = 0) -> dict:
    seeds = jax.random.split(jax.random.key(seed), 7)
    return {
        "train_act": scatter_about(seeds[0], (SEQS, SEQ_LEN, D), 0.106, 0.796875, ((0, 8), (1, 4), (2, 8))),
        "train_grad": scatter_about(seeds[1], (SEQS, SEQ_LEN, FF), 0.077, 0.59765625, ((0, 8), (1, 4), (2, 8))),
        "val_act": scatter_about(seeds[2], (VAL, D), 0.106, 0.796875, ((0, 8), (1, 8))),
        "val_grad": scatter_about(seeds[3], (VAL, FF), 0.077, 0.59765625, ((0, 8), (1, 8))),
        "val_mask": set_ends((jax.random.randint(seeds[4], (VAL,), 0, 8) < 7).astype(jnp.int32), jax.random.fold_in(seeds[4], 1), 0, 1),
        "lengths": set_ends(jax.random.randint(seeds[5], (SEQS,), SEQ_LEN // 4, SEQ_LEN + 1), jax.random.fold_in(seeds[5], 1), SEQ_LEN // 4, SEQ_LEN).astype(jnp.int32),
    }


def reference(train_act, train_grad, val_act, val_grad, val_mask, lengths):
    weights = val_mask.astype(jnp.float32)
    scale = float(val_act.shape[0]) ** (-0.5)
    positions = jnp.arange(train_act.shape[1]).astype(jnp.int32)

    def one_sequence(item):
        act, grad, length = item
        act_gram = jnp.dot(act, val_act.T, preferred_element_type=jnp.float32)
        grad_gram = jnp.dot(grad, val_grad.T, preferred_element_type=jnp.float32)
        values = lax.optimization_barrier(jnp.sum(act_gram * grad_gram * weights[None, :], axis=1)) * scale
        return jnp.where(positions < length, values, jnp.zeros_like(values))
    token_values = lax.map(one_sequence, (train_act, train_grad, lengths))
    example_values = lax.optimization_barrier(jnp.sum(token_values, axis=1)) / jnp.sqrt(lengths.astype(jnp.float32))
    return (token_values, example_values)
```

```python
import functools

import jax
import jax.numpy as jnp
from jax import lax
from jax.experimental import pallas as pl
from jax.experimental.pallas import tpu as pltpu
from jax.sharding import PartitionSpec as P

LANES = 128
EXTRA = 16
STEPS = 64.0
LARGEST = 32700.0
SMALLEST = 1e-33


def contract(left, right):
    return lax.dot_general(
        left, right, (((1,), (1,)), ((), ())), preferred_element_type=jnp.float32
    )


def encode(gram):
    top = jnp.max(jnp.abs(gram), axis=0, keepdims=True)
    step = jnp.ceil(jnp.log2(jnp.maximum(top, SMALLEST) * (1.0 / LARGEST)) * STEPS)
    codes = jnp.floor(gram * jnp.exp2(step * (-1.0 / STEPS)) + 0.5)
    return codes.astype(jnp.int32).astype(jnp.int16), step.astype(jnp.int32)


def gram_kernel(n_blocks, act_ref, grad_ref, *refs):
    block_refs, out_ref, val_ref = refs[:n_blocks], refs[n_blocks], refs[n_blocks + 1]
    count = val_ref.shape[0]
    width = act_ref.shape[1]

    @pl.when(pl.program_id(0) == 0)
    def _():
        start = 0
        for ref in block_refs:
            val_ref[start : start + ref.shape[0], :] = ref[...]
            start += ref.shape[0]

    act_codes, act_step = encode(contract(val_ref[:, :width], act_ref[...]))
    grad_codes, grad_step = encode(contract(val_ref[:, width:], grad_ref[...]))
    row = lax.broadcasted_iota(jnp.int32, (EXTRA, act_step.shape[1]), 0)
    steps = jnp.where(row == 0, act_step, grad_step).astype(jnp.int16)
    for peer in range(out_ref.shape[0]):
        lanes = slice(peer * LANES, (peer + 1) * LANES)
        out_ref[peer, :count, :] = act_codes[:, lanes]
        out_ref[peer, count : 2 * count, :] = grad_codes[:, lanes]
        out_ref[peer, 2 * count :, :] = steps[:, lanes]


def grams(train_act, train_grad, blocks):
    tokens, width = train_act.shape
    hidden = train_grad.shape[1]
    count = sum(block.shape[0] for block in blocks)
    tile = 2 * LANES
    return pl.pallas_call(
        functools.partial(gram_kernel, len(blocks)),
        grid=(tokens // tile,),
        out_shape=jax.ShapeDtypeStruct(
            (tokens // LANES, 2 * count + EXTRA, LANES), jnp.int16
        ),
        in_specs=[
            pl.BlockSpec((tile, width), lambda i: (i, 0)),
            pl.BlockSpec((tile, hidden), lambda i: (i, 0)),
        ]
        + [pl.BlockSpec(block.shape, lambda i: (0, 0)) for block in blocks],
        out_specs=pl.BlockSpec(
            (tile // LANES, 2 * count + EXTRA, LANES), lambda i: (i, 0, 0)
        ),
        scratch_shapes=[pltpu.VMEM((count, width + hidden), jnp.bfloat16)],
        compiler_params=pltpu.CompilerParams(vmem_limit_bytes=32 * 2**20),
        cost_estimate=pl.CostEstimate(
            flops=2 * tokens * count * (width + hidden),
            bytes_accessed=2 * (tokens + count) * (width + hidden),
            transcendentals=0,
        ),
    )(train_act, train_grad, *blocks)


def reduce_kernel(piece_ref, out_ref):
    peers, rows, _ = piece_ref.shape
    count = (rows - EXTRA) // 2

    def total(start, which):
        result = 0.0
        for peer in range(peers):
            step = piece_ref[peer, 2 * count :, :].astype(jnp.int32).astype(jnp.float32)
            scale = jnp.exp2(step[which : which + 1, :] * (1.0 / STEPS))
            codes = piece_ref[peer, start : start + count, :]
            result += codes.astype(jnp.int32).astype(jnp.float32) * scale
        return result

    out_ref[...] = jnp.sum(total(0, 0) * total(count, 1), axis=0, keepdims=True)


def reduce(pieces):
    return pl.pallas_call(
        reduce_kernel,
        out_shape=jax.ShapeDtypeStruct((1, LANES), jnp.float32),
        compiler_params=pltpu.CompilerParams(vmem_limit_bytes=32 * 2**20),
        cost_estimate=pl.CostEstimate(
            flops=4 * pieces.size, bytes_accessed=2 * pieces.size, transcendentals=0
        ),
    )(pieces)


def per_device(train_act, train_grad, val_act, val_grad, val_mask, lengths):
    _, piece, width = train_act.shape
    train_act = train_act.reshape(piece, width)
    train_grad = train_grad.reshape(piece, train_grad.shape[2])
    ring, groups, parts = (lax.axis_size(a) for a in ("dp", "tensor", "seq"))
    val_rows = val_act.shape[0]
    scale = float(val_rows * ring) ** (-0.5)

    mask = val_mask.astype(jnp.bfloat16)[:, None]
    own = jnp.concatenate([val_act * mask, val_grad * mask], axis=1)
    core = lax.axis_index("seq") % 2
    half = val_rows // 2
    own = jnp.where(core == 0, own, jnp.concatenate([own[half:], own[:half]], axis=0))
    along = []
    for place in range(ring):
        for part in range(parts):
            other = (place + (1 if part % 2 == 0 else -1)) % ring
            along.append((place * parts + part, other * parts + part))
    swap = [(part, part ^ 1) for part in range(parts)]

    def finish(blocks):
        codes = grams(train_act, train_grad, blocks)
        return reduce(lax.all_to_all(codes, "tensor", 0, 0, tiled=True))

    moving = lax.ppermute(own, ("dp", "seq"), along)
    values = finish([own])
    for distance in range(1, ring // 2 + 1):
        here = moving
        if distance + 1 < ring // 2:
            moving = lax.ppermute(here, ("dp", "seq"), along)
        elif distance + 1 == ring // 2:
            moving = lax.ppermute(here[:half], ("dp", "seq"), along)
        values += finish([here, lax.ppermute(here, "seq", swap)])

    everyone = jnp.broadcast_to(values * scale, (groups * parts, LANES))
    everyone = lax.all_to_all(everyone, ("tensor", "seq"), 0, 0, tiled=True)
    everyone = everyone.reshape(groups, parts, LANES).transpose(1, 0, 2)
    everyone = everyone.reshape(parts, piece)
    positions = jnp.arange(parts * piece).reshape(parts, piece)
    everyone = jnp.where(positions < lengths[0], everyone, jnp.zeros_like(everyone))
    token_values = lax.dynamic_slice_in_dim(everyone, lax.axis_index("seq"), 1, axis=0)
    example_values = jnp.sum(everyone)[None] / jnp.sqrt(lengths.astype(jnp.float32))
    return (token_values, example_values)


def solution(mesh):
    return jax.shard_map(
        per_device,
        mesh=mesh,
        in_specs=(
            P("dp", "seq", "tensor"),
            P("dp", "seq", "tensor"),
            P("dp", "tensor"),
            P("dp", "tensor"),
            P("dp"),
            P("dp"),
        ),
        out_specs=(P("dp", "seq"), P("dp")),
        check_vma=False,
    )
```

```python
import functools

import jax
import jax.numpy as jnp
from jax import lax
from jax.experimental import pallas as pl
from jax.experimental.pallas import tpu as pltpu
from jax.sharding import PartitionSpec as P

LANES = 128
TILE = 256
EXTRA = 16
STEPS = 64.0
LARGEST = 32700.0
SMALLEST = 1e-33
IN_VMEM = pl.BlockSpec(memory_space=pltpu.VMEM)
IN_SMEM = pl.BlockSpec(memory_space=pltpu.SMEM)


def kernel_call(
    kernel, name, out_shape, in_specs, out_specs, moved, scratch=(), grant=4
):
    return pl.pallas_call(
        kernel,
        name=name,
        out_shape=out_shape,
        in_specs=in_specs,
        out_specs=out_specs,
        scratch_shapes=scratch,
        compiler_params=pltpu.CompilerParams(vmem_limit_bytes=grant * 2**20),
        cost_estimate=pl.CostEstimate(flops=0, bytes_accessed=moved, transcendentals=0),
    )


def contract(left, right):
    return lax.dot_general(
        left, right, (((1,), (1,)), ((), ())), preferred_element_type=jnp.float32
    )


def prepare_kernel(core_ref, mask_in, act_in, grad_in, *refs):
    out_ref, mask_ref, act_ref, grad_ref, sems = refs
    copies = [
        pltpu.make_async_copy(source, target, sems.at[index])
        for index, (source, target) in enumerate(
            ((mask_in, mask_ref), (act_in, act_ref), (grad_in, grad_ref))
        )
    ]
    for copy in copies:
        copy.start()
    for copy in copies:
        copy.wait()
    rows, width = act_ref.shape
    half = rows // 2
    row = lax.broadcasted_iota(jnp.int32, (rows, rows), 0)
    column = lax.broadcasted_iota(jnp.int32, (rows, rows), 1)
    mask = jnp.where(row == column, mask_ref[...].astype(jnp.float32), 0.0)
    mask = jnp.sum(mask, axis=1, keepdims=True)
    for part in range(2):
        place = pl.multiple_of(jnp.where(core_ref[0] == part, 0, half), half)
        rows_in = slice(part * half, (part + 1) * half)
        factor = mask[rows_in].astype(jnp.bfloat16)
        out_ref[pl.ds(place, half), :width] = act_ref[rows_in, :] * factor
        out_ref[pl.ds(place, half), width:] = grad_ref[rows_in, :] * factor


def prepare(core, mask, act, grad):
    rows, width = act.shape
    shape = (rows, width + grad.shape[1])
    arrays = [pltpu.with_memory_space_constraint(a, pltpu.HBM) for a in (mask, act, grad)]
    return kernel_call(
        prepare_kernel,
        "prepare",
        jax.ShapeDtypeStruct(shape, act.dtype),
        [IN_SMEM] + [pl.BlockSpec(memory_space=pltpu.HBM)] * 3,
        IN_VMEM,
        8 * rows * shape[1],
        [pltpu.VMEM(a.shape, a.dtype) for a in arrays]
        + [pltpu.SemaphoreType.DMA((3,))],
        8,
    )(core, *arrays)


def encode(gram):
    top = jnp.max(jnp.abs(gram), axis=0, keepdims=True)
    step = jnp.ceil(jnp.log2(jnp.maximum(top, SMALLEST) * (1.0 / LARGEST)) * STEPS)
    codes = jnp.floor(gram * jnp.exp2(step * (-1.0 / STEPS)) + 0.5)
    return codes.astype(jnp.int32).astype(jnp.int16), step.astype(jnp.int32)


def gram_kernel(n_blocks, n_before, act_ref, grad_ref, *refs):
    block_refs, refs = refs[:n_blocks], refs[n_blocks:]
    before_refs, (out_ref, val_ref, code_ref, sems) = refs[:n_before], refs[n_before:]
    start = 0
    for ref in block_refs:
        val_ref[start : start + ref.shape[0], :] = ref[...]
        start += ref.shape[0]
    count = val_ref.shape[0]
    tokens, width = act_ref.shape
    each = TILE // LANES
    for ref in before_refs:
        code_ref[:, 2 * count + EXTRA :, :] = ref[...]
    copies = []
    for tile in range(tokens // TILE):
        rows = slice(tile * TILE, (tile + 1) * TILE)
        act_codes, act_step = encode(contract(val_ref[:, :width], act_ref[rows, :]))
        grad_codes, grad_step = encode(contract(val_ref[:, width:], grad_ref[rows, :]))
        row = lax.broadcasted_iota(jnp.int32, (EXTRA, TILE), 0)
        steps = jnp.where(row == 0, act_step, grad_step).astype(jnp.int16)
        for part in range(each):
            peer = tile * each + part
            lanes = slice(part * LANES, (part + 1) * LANES)
            code_ref[peer, :count, :] = act_codes[:, lanes]
            code_ref[peer, count : 2 * count, :] = grad_codes[:, lanes]
            code_ref[peer, 2 * count : 2 * count + EXTRA, :] = steps[:, lanes]
        peers = pl.ds(tile * each, each)
        copies.append(
            pltpu.make_async_copy(code_ref.at[peers], out_ref.at[peers], sems.at[tile])
        )
        copies[-1].start()
    for copy in copies:
        copy.wait()


def grams(train, blocks, before=(), place=pltpu.HBM):
    tokens = train[0].shape[0]
    width = train[0].shape[1] + train[1].shape[1]
    count = sum(block.shape[0] for block in blocks)
    rows = 2 * count + EXTRA + sum(codes.shape[1] for codes in before)
    shape = (tokens // LANES, rows, LANES)
    return kernel_call(
        functools.partial(gram_kernel, len(blocks), len(before)),
        "grams",
        place(shape, jnp.int16),
        [IN_VMEM] * (2 + len(blocks) + len(before)),
        pl.BlockSpec(memory_space=place),
        4 * tokens * count,
        [
            pltpu.VMEM((count, width), jnp.bfloat16),
            pltpu.VMEM(shape, jnp.int16),
            pltpu.SemaphoreType.DMA((tokens // TILE,)),
        ],
        12,
    )(*train, *blocks, *before)


def reduce_kernel(counts, scale, before_ref, piece_ref, out_ref):
    sums, start = before_ref[...], 0

    def total(first, count, which, steps):
        result = 0.0
        for peer in range(piece_ref.shape[0]):
            step = piece_ref[peer, steps : steps + EXTRA, :].astype(jnp.int32)
            step = step[which : which + 1, :].astype(jnp.float32)
            codes = piece_ref[peer, first : first + count, :]
            codes = codes.astype(jnp.int32).astype(jnp.float32)
            result += codes * jnp.exp2(step * (1.0 / STEPS))
        return result

    for count in counts:
        steps = start + 2 * count
        act = total(start, count, 0, steps)
        grad = total(start + count, count, 1, steps)
        sums += jnp.sum(act * grad, axis=0, keepdims=True)
        start = steps + EXTRA
    out_ref[...] = jnp.broadcast_to(sums * scale, out_ref.shape)


def reduce(before, pieces, counts, scale=1.0, copies=1):
    return kernel_call(
        functools.partial(reduce_kernel, counts, scale),
        "reduce",
        jax.ShapeDtypeStruct((copies, LANES), jnp.float32),
        [IN_VMEM, IN_VMEM],
        IN_VMEM,
        2 * pieces.size,
    )(before, pieces)


def finish_kernel(parts, seq_ref, length_ref, all_ref, token_ref, example_ref):
    rows = all_ref.shape[0]
    groups = rows // parts
    row = lax.broadcasted_iota(jnp.int32, (rows, LANES), 0)
    lane = lax.broadcasted_iota(jnp.int32, (rows, LANES), 1)
    position = ((row % parts) * groups + row // parts) * LANES + lane
    values = jnp.where(position < length_ref[0], all_ref[...], 0.0)
    for group in range(groups):
        group_values = values[group * parts : (group + 1) * parts]
        part = lax.broadcasted_iota(jnp.int32, (parts, LANES), 0)
        own = jnp.where(part == seq_ref[0], group_values, 0.0)
        token_ref[:, group * LANES : (group + 1) * LANES] = jnp.sum(
            own, axis=0, keepdims=True
        )
    total = jnp.sum(jnp.sum(values, axis=0, keepdims=True), axis=1, keepdims=True)
    length = jnp.full((1, 1), length_ref[0], jnp.int32).astype(jnp.float32)
    example_ref[0] = (total / jnp.sqrt(length))[0, 0]


def finish(parts, seq, lengths, everyone):
    return kernel_call(
        functools.partial(finish_kernel, parts),
        "finish",
        (
            jax.ShapeDtypeStruct((1, everyone.size // parts), jnp.float32),
            jax.ShapeDtypeStruct((1,), jnp.float32),
        ),
        [IN_SMEM, IN_SMEM, IN_VMEM],
        (IN_VMEM, IN_SMEM),
        4 * everyone.size,
    )(seq, lengths, everyone)


def per_device(train_act, train_grad, val_act, val_grad, val_mask, lengths):
    _, piece, width = train_act.shape
    train_act = train_act.reshape(piece, width)
    train_grad = train_grad.reshape(piece, train_grad.shape[2])
    ring, groups, parts = (lax.axis_size(a) for a in ("dp", "tensor", "seq"))
    val_rows = val_act.shape[0]
    scale = float(val_rows * ring) ** (-0.5)
    seq = lax.axis_index("seq").astype(jnp.int32).reshape(1)

    own = prepare(seq & 1, val_mask.reshape(1, val_rows), val_act, val_grad)
    own, half = [own], val_rows // 2
    along = []
    for place in range(ring):
        for part in range(parts):
            other = (place + (1 if part % 2 == 0 else -1)) % ring
            along.append((place * parts + part, other * parts + part))
    swap = [(part, part ^ 1) for part in range(parts)]

    def pass_on(blocks):
        return [lax.ppermute(block, ("dp", "seq"), along) for block in blocks]

    train = (train_act, train_grad)
    last = ring // 2
    moving = pass_on(own)
    codes = grams(train, own, (), pltpu.VMEM)
    own_codes, waiting, sent = codes, [], []
    for distance in range(1, last + 1):
        here, codes, own_codes = lax.optimization_barrier((moving, codes, own_codes))
        if distance < last - 2:
            moving = pass_on(here)
        elif distance == last - 2:
            moving = pass_on([here[0][:half], here[0][half:]])
        elif distance == last - 1:
            moving = pass_on(here[:1])
        waiting += here + [lax.ppermute(block, "seq", swap) for block in here]
        if distance == last - 1:
            continue
        counts, before = (sum(block.shape[0] for block in waiting),), ()
        if distance == 1:
            counts, before = counts + (val_rows,), (own_codes,)
        codes, waiting = grams(train, waiting, before), []
        sent.append((counts, lax.all_to_all(codes, "tensor", 0, 0, tiled=True)))
    values = jnp.zeros((1, LANES), jnp.float32)
    values, codes = lax.optimization_barrier((values, codes))
    for counts, pieces in sent[:-1]:
        values = reduce(values, pieces, counts)
    counts, pieces = sent[-1]
    everyone = reduce(values, pieces, counts, scale, groups * parts)

    everyone = lax.all_to_all(everyone, ("tensor", "seq"), 0, 0, tiled=True)
    return finish(parts, seq, lengths, everyone)


def solution(mesh):
    return jax.shard_map(
        per_device,
        mesh=mesh,
        in_specs=(
            P("dp", "seq", "tensor"),
            P("dp", "seq", "tensor"),
            P("dp", "tensor"),
            P("dp", "tensor"),
            P("dp"),
            P("dp"),
        ),
        out_specs=(P("dp", "seq"), P("dp")),
        check_vma=False,
    )
```

```python
import functools

import jax
import jax.numpy as jnp
from jax import lax
from jax.experimental import pallas as pl
from jax.experimental.pallas import tpu as pltpu
from jax.sharding import PartitionSpec as P

LANES = 128
TILE = 256
EXTRA = 16
STEPS = 64.0
LARGEST = 32700.0
SMALLEST = 1e-33
IN_VMEM = pl.BlockSpec(memory_space=pltpu.VMEM)
IN_SMEM = pl.BlockSpec(memory_space=pltpu.SMEM)


def kernel_call(
    kernel, name, out_shape, in_specs, out_specs, moved, scratch=(), grant=4
):
    return pl.pallas_call(
        kernel,
        name=name,
        out_shape=out_shape,
        in_specs=in_specs,
        out_specs=out_specs,
        scratch_shapes=scratch,
        compiler_params=pltpu.CompilerParams(vmem_limit_bytes=grant * 2**20),
        cost_estimate=pl.CostEstimate(flops=0, bytes_accessed=moved, transcendentals=0),
    )


def contract(left, right):
    return lax.dot_general(
        left, right, (((1,), (1,)), ((), ())), preferred_element_type=jnp.float32
    )


def prepare_kernel(core_ref, mask_in, act_in, grad_in, *refs):
    out_ref, mask_ref, act_ref, grad_ref, sems = refs
    copies = [
        pltpu.make_async_copy(source, target, sems.at[index])
        for index, (source, target) in enumerate(
            ((mask_in, mask_ref), (act_in, act_ref), (grad_in, grad_ref))
        )
    ]
    for copy in copies:
        copy.start()
    for copy in copies:
        copy.wait()
    rows, width = act_ref.shape
    half = rows // 2
    row = lax.broadcasted_iota(jnp.int32, (rows, rows), 0)
    column = lax.broadcasted_iota(jnp.int32, (rows, rows), 1)
    mask = jnp.where(row == column, mask_ref[...].astype(jnp.float32), 0.0)
    mask = jnp.sum(mask, axis=1, keepdims=True)
    for part in range(2):
        place = pl.multiple_of(jnp.where(core_ref[0] == part, 0, half), half)
        rows_in = slice(part * half, (part + 1) * half)
        factor = mask[rows_in].astype(jnp.bfloat16)
        out_ref[pl.ds(place, half), :width] = act_ref[rows_in, :] * factor
        out_ref[pl.ds(place, half), width:] = grad_ref[rows_in, :] * factor


def prepare(core, mask, act, grad):
    rows, width = act.shape
    shape = (rows, width + grad.shape[1])
    arrays = [pltpu.with_memory_space_constraint(a, pltpu.HBM) for a in (mask, act, grad)]
    return kernel_call(
        prepare_kernel,
        "prepare",
        jax.ShapeDtypeStruct(shape, act.dtype),
        [IN_SMEM] + [pl.BlockSpec(memory_space=pltpu.HBM)] * 3,
        IN_VMEM,
        8 * rows * shape[1],
        [pltpu.VMEM(a.shape, a.dtype) for a in arrays]
        + [pltpu.SemaphoreType.DMA((3,))],
        8,
    )(core, *arrays)


def load_kernel(source_ref, target_ref, sems):
    rows = source_ref.shape[0] // sems.shape[0]
    copies = []
    for part in range(sems.shape[0]):
        span = pl.ds(part * rows, rows)
        source, target = source_ref.at[span, :], target_ref.at[span, :]
        copies.append(pltpu.make_async_copy(source, target, sems.at[part]))
    for copy in copies:
        copy.start()
    for copy in copies:
        copy.wait()


def load(array):
    return kernel_call(
        load_kernel,
        "load",
        pltpu.VMEM(array.shape, array.dtype),
        [pl.BlockSpec(memory_space=pltpu.HBM)],
        IN_VMEM,
        4 * array.size,
        [pltpu.SemaphoreType.DMA((4,))],
    )(pltpu.with_memory_space_constraint(array, pltpu.HBM))


def encode(gram):
    top = jnp.max(jnp.abs(gram), axis=0, keepdims=True)
    step = jnp.ceil(jnp.log2(jnp.maximum(top, SMALLEST) * (1.0 / LARGEST)) * STEPS)
    codes = jnp.floor(gram * jnp.exp2(step * (-1.0 / STEPS)) + 0.5)
    return codes.astype(jnp.int32).astype(jnp.int16), step.astype(jnp.int32)


def gram_kernel(n_blocks, n_before, act_ref, grad_ref, *refs):
    block_refs, refs = refs[:n_blocks], refs[n_blocks:]
    before_refs, (out_ref, val_ref, code_ref, sems) = refs[:n_before], refs[n_before:]
    start = 0
    for ref in block_refs:
        val_ref[start : start + ref.shape[0], :] = ref[...]
        start += ref.shape[0]
    count = val_ref.shape[0]
    tokens, width = act_ref.shape
    each = TILE // LANES
    for ref in before_refs:
        code_ref[:, 2 * count + EXTRA :, :] = ref[...]
    copies = []
    for tile in range(tokens // TILE):
        rows = slice(tile * TILE, (tile + 1) * TILE)
        act_codes, act_step = encode(contract(val_ref[:, :width], act_ref[rows, :]))
        grad_codes, grad_step = encode(contract(val_ref[:, width:], grad_ref[rows, :]))
        row = lax.broadcasted_iota(jnp.int32, (EXTRA, TILE), 0)
        steps = jnp.where(row == 0, act_step, grad_step).astype(jnp.int16)
        for part in range(each):
            peer = tile * each + part
            lanes = slice(part * LANES, (part + 1) * LANES)
            code_ref[peer, :count, :] = act_codes[:, lanes]
            code_ref[peer, count : 2 * count, :] = grad_codes[:, lanes]
            code_ref[peer, 2 * count : 2 * count + EXTRA, :] = steps[:, lanes]
        peers = pl.ds(tile * each, each)
        copies.append(
            pltpu.make_async_copy(code_ref.at[peers], out_ref.at[peers], sems.at[tile])
        )
        copies[-1].start()
    for copy in copies:
        copy.wait()


def grams(train, blocks, before=(), place=pltpu.HBM):
    tokens = train[0].shape[0]
    width = train[0].shape[1] + train[1].shape[1]
    count = sum(block.shape[0] for block in blocks)
    rows = 2 * count + EXTRA + sum(codes.shape[1] for codes in before)
    shape = (tokens // LANES, rows, LANES)
    return kernel_call(
        functools.partial(gram_kernel, len(blocks), len(before)),
        "grams",
        place(shape, jnp.int16),
        [IN_VMEM] * (2 + len(blocks) + len(before)),
        pl.BlockSpec(memory_space=place),
        4 * tokens * count,
        [
            pltpu.VMEM((count, width), jnp.bfloat16),
            pltpu.VMEM(shape, jnp.int16),
            pltpu.SemaphoreType.DMA((tokens // TILE,)),
        ],
        12,
    )(*train, *blocks, *before)


def reduce_kernel(counts, scale, before_ref, piece_ref, out_ref):
    sums, start = before_ref[...], 0

    def total(first, count, which, steps):
        result = 0.0
        for peer in range(piece_ref.shape[0]):
            step = piece_ref[peer, steps : steps + EXTRA, :].astype(jnp.int32)
            step = step[which : which + 1, :].astype(jnp.float32)
            codes = piece_ref[peer, first : first + count, :]
            codes = codes.astype(jnp.int32).astype(jnp.float32)
            result += codes * jnp.exp2(step * (1.0 / STEPS))
        return result

    for count in counts:
        steps = start + 2 * count
        act = total(start, count, 0, steps)
        grad = total(start + count, count, 1, steps)
        sums += jnp.sum(act * grad, axis=0, keepdims=True)
        start = steps + EXTRA
    out_ref[...] = jnp.broadcast_to(sums * scale, out_ref.shape)


def reduce(before, pieces, counts, scale=1.0, copies=1):
    return kernel_call(
        functools.partial(reduce_kernel, counts, scale),
        "reduce",
        jax.ShapeDtypeStruct((copies, LANES), jnp.float32),
        [IN_VMEM, IN_VMEM],
        IN_VMEM,
        2 * pieces.size,
    )(before, pieces)


def finish_kernel(parts, seq_ref, length_ref, all_ref, token_ref, example_ref):
    rows = all_ref.shape[0]
    groups = rows // parts
    row = lax.broadcasted_iota(jnp.int32, (rows, LANES), 0)
    lane = lax.broadcasted_iota(jnp.int32, (rows, LANES), 1)
    position = ((row % parts) * groups + row // parts) * LANES + lane
    values = jnp.where(position < length_ref[0], all_ref[...], 0.0)
    for group in range(groups):
        group_values = values[group * parts : (group + 1) * parts]
        part = lax.broadcasted_iota(jnp.int32, (parts, LANES), 0)
        own = jnp.where(part == seq_ref[0], group_values, 0.0)
        token_ref[:, group * LANES : (group + 1) * LANES] = jnp.sum(
            own, axis=0, keepdims=True
        )
    total = jnp.sum(jnp.sum(values, axis=0, keepdims=True), axis=1, keepdims=True)
    length = jnp.full((1, 1), length_ref[0], jnp.int32).astype(jnp.float32)
    example_ref[0] = (total / jnp.sqrt(length))[0, 0]


def finish(parts, seq, lengths, everyone):
    return kernel_call(
        functools.partial(finish_kernel, parts),
        "finish",
        (
            jax.ShapeDtypeStruct((1, everyone.size // parts), jnp.float32),
            jax.ShapeDtypeStruct((1,), jnp.float32),
        ),
        [IN_SMEM, IN_SMEM, IN_VMEM],
        (IN_VMEM, IN_SMEM),
        4 * everyone.size,
    )(seq, lengths, everyone)


def per_device(train_act, train_grad, val_act, val_grad, val_mask, lengths):
    _, piece, width = train_act.shape
    train_act = train_act.reshape(piece, width)
    train_grad = train_grad.reshape(piece, train_grad.shape[2])
    ring, groups, parts = (lax.axis_size(a) for a in ("dp", "tensor", "seq"))
    val_rows = val_act.shape[0]
    scale = float(val_rows * ring) ** (-0.5)
    seq = lax.axis_index("seq").astype(jnp.int32).reshape(1)

    own = prepare(seq & 1, val_mask.reshape(1, val_rows), val_act, val_grad)
    own, half = [own], val_rows // 2
    along = []
    for place in range(ring):
        for part in range(parts):
            other = (place + (1 if part % 2 == 0 else -1)) % ring
            along.append((place * parts + part, other * parts + part))
    swap = [(part, part ^ 1) for part in range(parts)]

    def pass_on(blocks):
        return [lax.ppermute(block, ("dp", "seq"), along) for block in blocks]

    train = (train_act, train_grad)
    last = ring // 2
    moving = pass_on(own)
    codes = grams(train, own, (), pltpu.VMEM)
    own_codes, waiting, sent = codes, [], []
    for distance in range(1, last + 1):
        here, codes, own_codes = lax.optimization_barrier((moving, codes, own_codes))
        if distance < last - 2:
            moving = pass_on(here)
        elif distance == last - 2:
            moving = pass_on([here[0][:half], here[0][half:]])
        elif distance == last - 1:
            moving = pass_on(here[:1])
        waiting += here + [lax.ppermute(block, "seq", swap) for block in here]
        if distance == last:
            grad, _ = lax.optimization_barrier((train_grad, here[0]))
            train = (train_act, load(grad))
        if distance == last - 1:
            continue
        counts, before = (sum(block.shape[0] for block in waiting),), ()
        if distance == 1:
            counts, before = counts + (val_rows,), (own_codes,)
        codes, waiting = grams(train, waiting, before), []
        sent.append((counts, lax.all_to_all(codes, "tensor", 0, 0, tiled=True)))
    values = jnp.zeros((1, LANES), jnp.float32)
    values, codes = lax.optimization_barrier((values, codes))
    for counts, pieces in sent[:-1]:
        values = reduce(values, pieces, counts)
    counts, pieces = sent[-1]
    everyone = reduce(values, pieces, counts, scale, groups * parts)

    everyone = lax.all_to_all(everyone, ("tensor", "seq"), 0, 0, tiled=True)
    return finish(parts, seq, lengths, everyone)


def solution(mesh):
    return jax.shard_map(
        per_device,
        mesh=mesh,
        in_specs=(
            P("dp", "seq", "tensor"),
            P("dp", "seq", "tensor"),
            P("dp", "tensor"),
            P("dp", "tensor"),
            P("dp"),
            P("dp"),
        ),
        out_specs=(P("dp", "seq"), P("dp")),
        check_vma=False,
    )
```

```python
import functools

import jax
import jax.numpy as jnp
from jax import lax
from jax.experimental import pallas as pl
from jax.experimental.pallas import tpu as pltpu
from jax.sharding import PartitionSpec as P

LANES = 128
TILE = 256
EXTRA = 16
STEPS = 64.0
LARGEST = 32700.0
SMALLEST = 1e-33
IN_VMEM = pl.BlockSpec(memory_space=pltpu.VMEM)
IN_SMEM = pl.BlockSpec(memory_space=pltpu.SMEM)


def kernel_call(
    kernel, name, out_shape, in_specs, out_specs, moved, scratch=(), grant=4, aliases=None
):
    return pl.pallas_call(
        kernel,
        name=name,
        out_shape=out_shape,
        in_specs=in_specs,
        out_specs=out_specs,
        scratch_shapes=scratch,
        input_output_aliases=aliases or {},
        compiler_params=pltpu.CompilerParams(vmem_limit_bytes=grant * 2**20),
        cost_estimate=pl.CostEstimate(flops=0, bytes_accessed=moved, transcendentals=0),
    )


def contract(left, right):
    return lax.dot_general(
        left, right, (((1,), (1,)), ((), ())), preferred_element_type=jnp.float32
    )


def prepare_kernel(core_ref, mask_in, act_in, grad_in, *refs):
    out_ref, mask_ref, act_ref, grad_ref, sems = refs
    copies = [
        pltpu.make_async_copy(source, target, sems.at[index])
        for index, (source, target) in enumerate(
            ((mask_in, mask_ref), (act_in, act_ref), (grad_in, grad_ref))
        )
    ]
    for copy in copies:
        copy.start()
    for copy in copies:
        copy.wait()
    rows, width = act_ref.shape
    half = rows // 2
    row = lax.broadcasted_iota(jnp.int32, (rows, rows), 0)
    column = lax.broadcasted_iota(jnp.int32, (rows, rows), 1)
    mask = jnp.where(row == column, mask_ref[...].astype(jnp.float32), 0.0)
    mask = jnp.sum(mask, axis=1, keepdims=True)
    for part in range(2):
        place = pl.multiple_of(jnp.where(core_ref[0] == part, 0, half), half)
        rows_in = slice(part * half, (part + 1) * half)
        factor = mask[rows_in].astype(jnp.bfloat16)
        out_ref[pl.ds(place, half), :width] = act_ref[rows_in, :] * factor
        out_ref[pl.ds(place, half), width:] = grad_ref[rows_in, :] * factor


def prepare(core, mask, act, grad):
    rows, width = act.shape
    shape = (rows, width + grad.shape[1])
    arrays = [pltpu.with_memory_space_constraint(a, pltpu.HBM) for a in (mask, act, grad)]
    return kernel_call(
        prepare_kernel,
        "prepare",
        jax.ShapeDtypeStruct(shape, act.dtype),
        [IN_SMEM] + [pl.BlockSpec(memory_space=pltpu.HBM)] * 3,
        IN_VMEM,
        8 * rows * shape[1],
        [pltpu.VMEM(a.shape, a.dtype) for a in arrays]
        + [pltpu.SemaphoreType.DMA((3,))],
        8,
    )(core, *arrays)


def load_kernel(source_ref, target_ref, sems):
    rows = source_ref.shape[0] // sems.shape[0]
    copies = []
    for part in range(sems.shape[0]):
        span = pl.ds(part * rows, rows)
        source, target = source_ref.at[span, :], target_ref.at[span, :]
        copies.append(pltpu.make_async_copy(source, target, sems.at[part]))
    for copy in copies:
        copy.start()
    for copy in copies:
        copy.wait()


def load(array):
    return kernel_call(
        load_kernel,
        "load",
        pltpu.VMEM(array.shape, array.dtype),
        [pl.BlockSpec(memory_space=pltpu.HBM)],
        IN_VMEM,
        4 * array.size,
        [pltpu.SemaphoreType.DMA((4,))],
    )(pltpu.with_memory_space_constraint(array, pltpu.HBM))


def encode(gram):
    top = jnp.max(jnp.abs(gram), axis=0, keepdims=True)
    step = jnp.ceil(jnp.log2(jnp.maximum(top, SMALLEST) * (1.0 / LARGEST)) * STEPS)
    codes = jnp.floor(gram * jnp.exp2(step * (-1.0 / STEPS)) + 0.5)
    return codes.astype(jnp.int32).astype(jnp.int16), step.astype(jnp.int32)


def gram_kernel(n_blocks, first, act_ref, grad_ref, *refs):
    block_refs, (out_ref, val_ref, code_ref, sems) = refs[:n_blocks], refs[-4:]
    start = 0
    for ref in block_refs:
        val_ref[start : start + ref.shape[0], :] = ref[...]
        start += ref.shape[0]
    count = val_ref.shape[0]
    tokens, width = act_ref.shape
    each = TILE // LANES
    span = pl.ds(first, 2 * count + EXTRA)
    copies = []
    for tile in range(tokens // TILE):
        rows = slice(tile * TILE, (tile + 1) * TILE)
        act_codes, act_step = encode(contract(val_ref[:, :width], act_ref[rows, :]))
        grad_codes, grad_step = encode(contract(val_ref[:, width:], grad_ref[rows, :]))
        row = lax.broadcasted_iota(jnp.int32, (EXTRA, TILE), 0)
        steps = jnp.where(row == 0, act_step, grad_step).astype(jnp.int16)
        for part in range(each):
            peer = tile * each + part
            lanes = slice(part * LANES, (part + 1) * LANES)
            code_ref[peer, :count, :] = act_codes[:, lanes]
            code_ref[peer, count : 2 * count, :] = grad_codes[:, lanes]
            code_ref[peer, 2 * count : 2 * count + EXTRA, :] = steps[:, lanes]
        peers = pl.ds(tile * each, each)
        copies.append(
            pltpu.make_async_copy(
                code_ref.at[peers], out_ref.at[peers, span, :], sems.at[tile]
            )
        )
        copies[-1].start()
    for copy in copies:
        copy.wait()


def grams(train, blocks, first=0, shared=()):
    tokens = train[0].shape[0]
    width = train[0].shape[1] + train[1].shape[1]
    count = sum(block.shape[0] for block in blocks)
    rows = 2 * count + EXTRA
    shape = (tokens // LANES, rows, LANES)
    in_hbm = pl.BlockSpec(memory_space=pltpu.HBM)
    whole = shared[0].shape if shared else (shape[0], first + rows, LANES)
    return kernel_call(
        functools.partial(gram_kernel, len(blocks), first),
        "grams",
        pltpu.HBM(whole, jnp.int16),
        [IN_VMEM] * (2 + len(blocks)) + [in_hbm] * len(shared),
        in_hbm,
        4 * tokens * count,
        [
            pltpu.VMEM((count, width), jnp.bfloat16),
            pltpu.VMEM(shape, jnp.int16),
            pltpu.SemaphoreType.DMA((tokens // TILE,)),
        ],
        12,
        {2 + len(blocks): 0} if shared else None,
    )(*train, *blocks, *shared)


def reduce_kernel(counts, scale, before_ref, piece_ref, out_ref):
    sums, start = before_ref[...], 0

    def total(first, count, which, steps):
        result = 0.0
        for peer in range(piece_ref.shape[0]):
            step = piece_ref[peer, steps : steps + EXTRA, :].astype(jnp.int32)
            step = step[which : which + 1, :].astype(jnp.float32)
            codes = piece_ref[peer, first : first + count, :]
            codes = codes.astype(jnp.int32).astype(jnp.float32)
            result += codes * jnp.exp2(step * (1.0 / STEPS))
        return result

    for count in counts:
        steps = start + 2 * count
        act = total(start, count, 0, steps)
        grad = total(start + count, count, 1, steps)
        sums += jnp.sum(act * grad, axis=0, keepdims=True)
        start = steps + EXTRA
    out_ref[...] = jnp.broadcast_to(sums * scale, out_ref.shape)


def reduce(before, pieces, counts, scale=1.0, copies=1):
    return kernel_call(
        functools.partial(reduce_kernel, counts, scale),
        "reduce",
        jax.ShapeDtypeStruct((copies, LANES), jnp.float32),
        [IN_VMEM, IN_VMEM],
        IN_VMEM,
        2 * pieces.size,
    )(before, pieces)


def finish_kernel(parts, seq_ref, length_ref, all_ref, token_ref, example_ref):
    rows = all_ref.shape[0]
    groups = rows // parts
    row = lax.broadcasted_iota(jnp.int32, (rows, LANES), 0)
    lane = lax.broadcasted_iota(jnp.int32, (rows, LANES), 1)
    position = ((row % parts) * groups + row // parts) * LANES + lane
    values = jnp.where(position < length_ref[0], all_ref[...], 0.0)
    for group in range(groups):
        group_values = values[group * parts : (group + 1) * parts]
        part = lax.broadcasted_iota(jnp.int32, (parts, LANES), 0)
        own = jnp.where(part == seq_ref[0], group_values, 0.0)
        token_ref[:, group * LANES : (group + 1) * LANES] = jnp.sum(
            own, axis=0, keepdims=True
        )
    total = jnp.sum(jnp.sum(values, axis=0, keepdims=True), axis=1, keepdims=True)
    length = jnp.full((1, 1), length_ref[0], jnp.int32).astype(jnp.float32)
    example_ref[0] = (total / jnp.sqrt(length))[0, 0]


def finish(parts, seq, lengths, everyone):
    return kernel_call(
        functools.partial(finish_kernel, parts),
        "finish",
        (
            jax.ShapeDtypeStruct((1, everyone.size // parts), jnp.float32),
            jax.ShapeDtypeStruct((1,), jnp.float32),
        ),
        [IN_SMEM, IN_SMEM, IN_VMEM],
        (IN_VMEM, IN_SMEM),
        4 * everyone.size,
    )(seq, lengths, everyone)


def per_device(train_act, train_grad, val_act, val_grad, val_mask, lengths):
    _, piece, width = train_act.shape
    train_act = train_act.reshape(piece, width)
    train_grad = train_grad.reshape(piece, train_grad.shape[2])
    ring, groups, parts = (lax.axis_size(a) for a in ("dp", "tensor", "seq"))
    val_rows = val_act.shape[0]
    scale = float(val_rows * ring) ** (-0.5)
    seq = lax.axis_index("seq").astype(jnp.int32).reshape(1)

    own = prepare(seq & 1, val_mask.reshape(1, val_rows), val_act, val_grad)
    own, half = [own], val_rows // 2
    along = []
    for place in range(ring):
        for part in range(parts):
            other = (place + (1 if part % 2 == 0 else -1)) % ring
            along.append((place * parts + part, other * parts + part))
    swap = [(part, part ^ 1) for part in range(parts)]

    def pass_on(blocks):
        return [lax.ppermute(block, ("dp", "seq"), along) for block in blocks]

    train = (train_act, train_grad)
    last = ring // 2
    moving = pass_on(own)
    codes = grams(train, own, 4 * val_rows + EXTRA)
    waiting, sent = [], []
    for distance in range(1, last + 1):
        here, codes = lax.optimization_barrier((moving, codes))
        if distance == 1:
            own_codes = codes
        if distance < last - 2:
            moving = pass_on(here)
        elif distance == last - 2:
            moving = pass_on([here[0][:half], here[0][half:]])
        elif distance == last - 1:
            moving = pass_on(here[:1])
        waiting += here + [lax.ppermute(block, "seq", swap) for block in here]
        if distance == last:
            grad, _ = lax.optimization_barrier((train_grad, here[0]))
            train = (train_act, load(grad))
        if distance == last - 1:
            continue
        counts, shared = (sum(block.shape[0] for block in waiting),), ()
        if distance == 1:
            counts, shared = counts + (val_rows,), (own_codes,)
        codes, waiting = grams(train, waiting, 0, shared), []
        sent.append((counts, lax.all_to_all(codes, "tensor", 0, 0, tiled=True)))
    values = jnp.zeros((1, LANES), jnp.float32)
    values, codes = lax.optimization_barrier((values, codes))
    for counts, pieces in sent[:-1]:
        values = reduce(values, pieces, counts)
    counts, pieces = sent[-1]
    everyone = reduce(values, pieces, counts, scale, groups * parts)

    everyone = lax.all_to_all(everyone, ("tensor", "seq"), 0, 0, tiled=True)
    return finish(parts, seq, lengths, everyone)


def solution(mesh):
    return jax.shard_map(
        per_device,
        mesh=mesh,
        in_specs=(
            P("dp", "seq", "tensor"),
            P("dp", "seq", "tensor"),
            P("dp", "tensor"),
            P("dp", "tensor"),
            P("dp"),
            P("dp"),
        ),
        out_specs=(P("dp", "seq"), P("dp")),
        check_vma=False,
    )
```
